32 devices in a mesh: path: 8 (over y, x, core), tensor: 4 (over z).
Axes of the slice: x: 2, y: 2, z: 4, core: 2. Of those that a mesh axis runs over, the one named last changes fastest.
Arguments:
- hidden_in: bfloat16 [3072, 2048], P(('path', 'tensor')), may hold values from -120 to 120
- teacher: bfloat16 [3072, 2048], P('path'), may hold values from -3 to 3
- params: bfloat16 [3, 3, 7168, 2048], P(None, None, ('tensor', 'path')), may hold values from -4 to 4
- momentum: float32 [3, 3, 7168, 2048], P(None, None, ('tensor', 'path')), may hold values from -3 to 3
- path_alive: int32 [8], replicated, may hold values from 0 to 1, as said below
- path_module: int32 [8], replicated, may hold values from 0 to 2, as said below
Outputs:
- new_params: bfloat16 [3, 3, 7168, 2048], P(None, None, ('tensor', 'path'))
- new_momentum: float32 [3, 3, 7168, 2048], P(None, None, ('tensor', 'path'))
The draws below stay inside these ranges and needn't reach their ends.
Inputs may be any that keep to these rules, and one draw needn't show every extreme that they name: `path_alive`: at least one path is dead. `path_module`: every one of the 3 modules is used by at least one path whose path_alive entry is 1.
All inputs are finite; a program needn't handle non-finite values.
Results may differ from the reference program's by a relative error of at most 0.0047.
Values may be sent and summed in bfloat16 or wider, within the bound.
A program may use at most 128 MiB of HBM per device.

```python
import math
import jax
import jax.numpy as jnp
from jax import lax

D = 2048
FW = 7168
TOK = 384
MODS = 3
PATHS = 8


def draw_hidden_in(key, part):
    keys = jax.random.split(key, 3)
    row_count = PATHS * TOK
    row_scale = jnp.exp(jax.random.uniform(keys[0], (row_count, 1), jnp.float32, 0.0, math.log(10.0)))
    col_scale = jnp.exp(jax.random.uniform(keys[1], (1, D), jnp.float32, 0.0, math.log(3.0)))
    values = jnp.clip(jax.random.normal(keys[2], (row_count, D), jnp.float32), -4.0, 4.0) * row_scale * col_scale
    return values.astype(jnp.bfloat16)


def path_tables(key):
    base_key = jax.random.fold_in(key, 101)
    keys = jax.random.split(base_key, 4)
    levels = jax.random.randint(keys[0], (PATHS,), 1, 2 ** MODS)
    ranking = jnp.zeros((PATHS,), jnp.int32)
    for bit_pos in range(1, MODS):
        ranking = ranking + (levels >= 2 ** bit_pos).astype(jnp.int32)
    ordering = jax.random.permutation(keys[1], MODS).astype(jnp.int32)
    module = jnp.take(ordering, ranking)
    anchors = jax.random.permutation(keys[2], PATHS).astype(jnp.int32)
    chosen = anchors[:MODS]
    module = module.at[chosen].set(jnp.arange(MODS, dtype=jnp.int32))
    alive_flags = (jax.random.randint(keys[3], (PATHS,), 0, 4) > 0).astype(jnp.int32)
    alive_flags = alive_flags.at[chosen].set(1)
    alive_flags = alive_flags.at[anchors[MODS]].set(0)
    return (alive_flags, module.astype(jnp.int32))


def draw_path_alive(key, part):
    return path_tables(key)[0]


def draw_path_module(key, part):
    return path_tables(key)[1]


def block_scale(stream_key, dims, cuts, smallest, high):
    loudness = 1.0
    for dim, parts in cuts:
        draws = jax.random.uniform(jax.random.fold_in(jax.random.fold_in(stream_key, 6), dim), (parts,), jnp.float32, smallest / len(cuts), high / len(cuts))
        loudness = loudness * jnp.repeat(jnp.exp(draws), dims[dim] // parts).reshape((-1,) + (1,) * (len(dims) - 1 - dim))
    return loudness


def normal_values(key, extent, scale, reach, cuts=(), kind=jnp.bfloat16):
    loudness = block_scale(key, extent, cuts, -0.22, 0.18) if cuts else 1.0
    array = jax.random.normal(key, extent, jnp.float32) * scale * loudness
    return jnp.minimum(jnp.maximum(array, -reach), reach).astype(kind)


def setup_inputs(seed: int = 0) -> dict:
    arg_keys = jax.random.split(jax.random.key(seed), 7)
    hidden_in = draw_hidden_in(jax.random.fold_in(arg_keys[6], 71), 0)
    teacher = normal_values(arg_keys[1], (PATHS * TOK, D), 0.5, 3.0, ((0, 8),))
    params = normal_values(arg_keys[2], (MODS, 3, FW, D), 1.0, 4.0, ((2, 32),))
    momentum = normal_values(arg_keys[3], (MODS, 3, FW, D), 0.5, 3.0, ((2, 32),), jnp.float32)
    path_alive = draw_path_alive(jax.random.fold_in(arg_keys[6], 71), 0)
    path_module = draw_path_module(jax.random.fold_in(arg_keys[6], 71), 0)
    return {"hidden_in": hidden_in, "teacher": teacher, "params": params, "momentum": momentum, "path_alive": path_alive, "path_module": path_module}


def path_delta(rows_in, target, weights):
    mean_sq = lax.optimization_barrier(jnp.mean(jnp.square(rows_in.astype(jnp.float32)), axis=1, keepdims=True))
    normed = (rows_in.astype(jnp.float32) * lax.rsqrt(mean_sq + 1e-05)).astype(jnp.bfloat16)
    gate_pre = jnp.dot(normed, weights[0].T, preferred_element_type=jnp.float32) / math.sqrt(D)
    up_proj = jnp.dot(normed, weights[1].T, preferred_element_type=jnp.float32) / math.sqrt(D)
    sigmoid_gate = jax.nn.sigmoid(gate_pre)
    activated = gate_pre * sigmoid_gate
    hidden = (activated * up_proj).astype(jnp.bfloat16)
    output = jnp.dot(hidden, weights[2], preferred_element_type=jnp.float32) / math.sqrt(FW)
    cotangent = (4.0 * (output - target.astype(jnp.float32))).astype(jnp.bfloat16)
    hidden_grad = jnp.dot(cotangent, weights[2].T, preferred_element_type=jnp.float32) / math.sqrt(FW)
    gate_grad = (hidden_grad * up_proj * sigmoid_gate * (1.0 + gate_pre * (1.0 - sigmoid_gate))).astype(jnp.bfloat16)
    up_grad = (hidden_grad * activated).astype(jnp.bfloat16)
    gate_delta = (jnp.dot(gate_grad.T, normed, preferred_element_type=jnp.float32) / math.sqrt(D)).astype(jnp.bfloat16)
    up_delta = (jnp.dot(up_grad.T, normed, preferred_element_type=jnp.float32) / math.sqrt(D)).astype(jnp.bfloat16)
    down_delta = (jnp.dot(hidden.T, cotangent, preferred_element_type=jnp.float32) / math.sqrt(FW)).astype(jnp.bfloat16)
    return jnp.stack([gate_delta, up_delta, down_delta])

def reference(hidden_in, teacher, params, momentum, path_alive, path_module):

    def accumulate(state_pair, which):
        summed, counts = state_pair
        module = path_module[which]
        start = (which * TOK).astype(jnp.int32)
        rows_in = lax.dynamic_slice_in_dim(hidden_in, start, TOK, 0)
        target = lax.dynamic_slice_in_dim(teacher, start, TOK, 0)
        weights = lax.dynamic_index_in_dim(params, module, 0, keepdims=False)
        pseudo_grad = path_delta(rows_in, target, weights)
        is_alive = path_alive[which].astype(jnp.float32)
        current = lax.dynamic_index_in_dim(summed, module, 0, keepdims=False)
        summed = lax.dynamic_update_index_in_dim(summed, current + is_alive * pseudo_grad.astype(jnp.float32), module, 0)
        counts = counts + is_alive * (jnp.arange(MODS, dtype=jnp.int32) == module).astype(jnp.float32)
        return ((summed, counts), None)
    initial = (jnp.zeros(params.shape, jnp.float32), jnp.zeros((MODS,), jnp.float32))
    (summed, counts), _ = lax.scan(accumulate, initial, jnp.arange(PATHS, dtype=jnp.int32))
    mean_delta = summed / counts[:, None, None, None]
    new_momentum = 0.9 * momentum + mean_delta
    new_params = (params.astype(jnp.float32) - 0.7 * (mean_delta + 0.9 * new_momentum)).astype(jnp.bfloat16)
    return (new_params, new_momentum)
```

```python
import math

import jax
import jax.numpy as jnp
from jax import lax
from jax.experimental import pallas as pl
from jax.experimental.pallas import tpu as pltpu
from jax.sharding import PartitionSpec as P

D = 2048
FW = 7168
NT = (((1,), (1,)), ((), ()))
TN = (((0,), (0,)), ((), ()))
BOTH = ("path", "tensor")
EACH_VMEM = 56 * 1024 * 1024


def rms(rows):
    wide = rows.astype(jnp.float32)
    mean_sq = jnp.mean(jnp.square(wide), axis=1, keepdims=True)
    return (wide * lax.rsqrt(mean_sq + 1e-05)).astype(jnp.bfloat16)


def forward_kernel(order, module, z_ref, w_ref, part_ref, gate_ref, up_ref):
    z = z_ref[...]
    gate = lax.dot_general(w_ref[0, 0], z, NT, preferred_element_type=jnp.float32) / math.sqrt(D)
    up = lax.dot_general(w_ref[0, 1], z, NT, preferred_element_type=jnp.float32) / math.sqrt(D)
    gate_ref[0] = gate
    up_ref[0] = up
    hidden = (gate * jax.nn.sigmoid(gate) * up).astype(jnp.bfloat16)
    out = lax.dot_general(hidden, w_ref[0, 2], TN, preferred_element_type=jnp.float32)
    part_ref[...] = (out / math.sqrt(FW)).astype(part_ref.dtype)


def forward(order, module, normed, params):
    paths = order.shape[0]
    tok = normed.shape[0] // paths
    _, kinds, rows, width = params.shape
    saved = jax.ShapeDtypeStruct((paths, rows, tok), jnp.float32)
    saved_spec = pl.BlockSpec((1, rows, tok), lambda j, o, m: (o[j], 0, 0))
    return pl.pallas_call(
        forward_kernel,
        grid_spec=pltpu.PrefetchScalarGridSpec(
            num_scalar_prefetch=2,
            grid=(paths,),
            in_specs=[
                pl.BlockSpec((tok, width), lambda j, o, m: (o[j], 0)),
                pl.BlockSpec((1, kinds, rows, width), lambda j, o, m: (m[j], 0, 0, 0)),
            ],
            out_specs=[
                pl.BlockSpec((tok, width), lambda j, o, m: (o[j], 0)),
                saved_spec,
                saved_spec,
            ],
        ),
        out_shape=[
            jax.ShapeDtypeStruct((paths * tok, width), PART),
            saved,
            saved,
        ],
        compiler_params=pltpu.CompilerParams(vmem_limit_bytes=EACH_VMEM),
    )(order, module, normed, params)


def backward_kernel(
    order, module, alive, first, last, scale,
    z_ref, cot_ref, gate_ref, up_ref, w_ref, mom_ref, new_w_ref, new_mom_ref, total,
):
    j = pl.program_id(0)

    @pl.when(first[j] == 1)
    def _():
        total[...] = jnp.zeros_like(total)

    @pl.when(alive[j] == 1)
    def _():
        z = z_ref[...]
        cot = cot_ref[...]
        gate = gate_ref[0]
        up = up_ref[0]
        grad = lax.dot_general(w_ref[0, 2], cot, NT, preferred_element_type=jnp.float32)
        grad = grad / math.sqrt(FW)
        sig = jax.nn.sigmoid(gate)
        act = gate * sig
        gate_grad = (grad * up * sig * (1.0 + gate * (1.0 - sig))).astype(jnp.bfloat16)
        up_grad = (grad * act).astype(jnp.bfloat16)
        hidden = (act * up).astype(jnp.bfloat16)

        def add(kind, left, right, factor):
            delta = jnp.dot(left, right, preferred_element_type=jnp.float32) / factor
            total[kind] += delta.astype(jnp.bfloat16).astype(jnp.float32)

        add(0, gate_grad, z, math.sqrt(D))
        add(1, up_grad, z, math.sqrt(D))
        add(2, hidden, cot, math.sqrt(FW))

    @pl.when(last[j] == 1)
    def _():
        mean = total[...] / scale[module[j]]
        new_mom = 0.9 * mom_ref[0] + mean
        new_mom_ref[0] = new_mom
        new_w_ref[0] = (w_ref[0].astype(jnp.float32) - 0.7 * (mean + 0.9 * new_mom)).astype(
            jnp.bfloat16
        )


def backward(order, module, alive, first, last, counts, normed, cot, gate, up, params, momentum):
    paths = order.shape[0]
    tok = normed.shape[0] // paths
    _, kinds, rows, width = params.shape
    row_spec = pl.BlockSpec((tok, width), lambda j, o, m, *_: (o[j], 0))
    saved_spec = pl.BlockSpec((1, rows, tok), lambda j, o, m, *_: (o[j], 0, 0))
    own_spec = pl.BlockSpec((1, kinds, rows, width), lambda j, o, m, *_: (m[j], 0, 0, 0))
    return pl.pallas_call(
        backward_kernel,
        grid_spec=pltpu.PrefetchScalarGridSpec(
            num_scalar_prefetch=6,
            grid=(paths,),
            in_specs=[row_spec, row_spec, saved_spec, saved_spec, own_spec, own_spec],
            out_specs=[own_spec, own_spec],
            scratch_shapes=[pltpu.VMEM((kinds, rows, width), jnp.float32)],
        ),
        out_shape=[
            jax.ShapeDtypeStruct(params.shape, jnp.bfloat16),
            jax.ShapeDtypeStruct(momentum.shape, jnp.float32),
        ],
        compiler_params=pltpu.CompilerParams(vmem_limit_bytes=EACH_VMEM),
    )(order, module, alive, first, last, counts, normed, cot, gate, up, params, momentum)


PART = jnp.bfloat16


def plan_order(path_alive, path_module, module_count):
    paths = path_alive.shape[0]
    index = jnp.arange(paths, dtype=jnp.int32)
    key = path_module * paths + index
    rank = jnp.sum((key[None, :] < key[:, None]).astype(jnp.int32), axis=1)
    at = (rank[None, :] == index[:, None]).astype(jnp.int32)
    order = jnp.sum(at * index[None, :], axis=1)
    module = jnp.sum(at * path_module[None, :], axis=1)
    alive = jnp.sum(at * path_alive[None, :], axis=1)
    edge = jnp.ones((1,), jnp.int32)
    change = (module[1:] != module[:-1]).astype(jnp.int32)
    first = jnp.concatenate([edge, change])
    last = jnp.concatenate([change, edge])
    member = (path_module[:, None] == jnp.arange(module_count, dtype=jnp.int32)[None, :]).astype(
        jnp.int32
    ) * path_alive[:, None]
    counts = jnp.sum(member, axis=0).astype(jnp.float32)
    return order, module, alive, first, last, counts


def tokens_move(hidden_in, teacher, params, momentum, path_alive, path_module):
    order, module, alive, first, last, counts = plan_order(
        path_alive, path_module, params.shape[0]
    )
    share = hidden_in.shape[0]
    normed = lax.all_gather(rms(hidden_in), BOTH, axis=0, tiled=True)
    part, gate, up = forward(order, module, normed, params)
    output = lax.psum_scatter(part, BOTH, scatter_dimension=0, tiled=True)
    own = lax.dynamic_slice_in_dim(teacher, lax.axis_index("tensor") * share, share, 0)
    cot_share = (4.0 * (output.astype(jnp.float32) - own.astype(jnp.float32))).astype(jnp.bfloat16)
    cot = lax.all_gather(cot_share, BOTH, axis=0, tiled=True)
    return tuple(
        backward(
            order, module, alive, first, last, counts, normed, cot, gate, up, params, momentum
        )
    )


def module_sums(weighting, received):
    flat = received.reshape(received.shape[0], -1)
    return lax.dot_general(weighting, flat, TN, preferred_element_type=jnp.float32)


def pick(stacked, path_module):
    index = path_module[:, None, None]
    chosen = jnp.broadcast_to(stacked[0][None], (path_module.shape[0],) + stacked.shape[1:])
    for m in range(1, stacked.shape[0]):
        chosen = jnp.where(index == m, stacked[m][None], chosen)
    return chosen


def weights_move(hidden_in, teacher, params, momentum, path_alive, path_module):
    module_count = params.shape[0]
    block_rows = params.shape[2]
    width = params.shape[3]
    path_count = path_alive.shape[0]
    n_tensor = lax.axis_size("tensor")

    def to_paths(x):
        return lax.all_to_all(x, "path", split_axis=0, concat_axis=0, tiled=True)

    local_rows = path_count * block_rows
    gate_rows, up_rows, down_rows = (
        to_paths(pick(params[:, k], path_module)).reshape(local_rows, width) for k in range(3)
    )
    normed = rms(lax.all_gather(hidden_in, "tensor", axis=0, tiled=True))
    gate_pre = lax.dot_general(
        normed, gate_rows, NT, preferred_element_type=jnp.float32
    ) / math.sqrt(D)
    up_proj = lax.dot_general(normed, up_rows, NT, preferred_element_type=jnp.float32) / math.sqrt(
        D
    )
    sigmoid_gate = jax.nn.sigmoid(gate_pre)
    activated = gate_pre * sigmoid_gate
    hidden = (activated * up_proj).astype(jnp.bfloat16)
    share_rows = teacher.shape[0] // n_tensor
    output_share = lax.psum_scatter(
        jnp.dot(hidden, down_rows, preferred_element_type=jnp.float32) / math.sqrt(FW),
        "tensor",
        scatter_dimension=0,
        tiled=True,
    )
    own_rows = lax.dynamic_slice_in_dim(
        teacher, lax.axis_index("tensor") * share_rows, share_rows, 0
    )
    cotangent_share = (4.0 * (output_share - own_rows.astype(jnp.float32))).astype(jnp.bfloat16)
    cotangent = lax.all_gather(cotangent_share, "tensor", axis=0, tiled=True)
    down_delta = (
        lax.dot_general(hidden, cotangent, TN, preferred_element_type=jnp.float32) / math.sqrt(FW)
    ).astype(jnp.bfloat16)
    hidden_grad = lax.dot_general(
        cotangent, down_rows, NT, preferred_element_type=jnp.float32
    ) / math.sqrt(FW)
    gate_grad = (
        hidden_grad * up_proj * sigmoid_gate * (1.0 + gate_pre * (1.0 - sigmoid_gate))
    ).astype(jnp.bfloat16)
    up_grad = (hidden_grad * activated).astype(jnp.bfloat16)
    member = (path_module[:, None] == jnp.arange(module_count, dtype=jnp.int32)[None, :]).astype(
        jnp.int32
    ) * path_alive[:, None]
    weighting = member.astype(jnp.bfloat16)
    counts = jnp.sum(member, axis=0).astype(jnp.float32)
    piece_shape = (path_count, block_rows, width)
    gate_delta = (
        lax.dot_general(gate_grad, normed, TN, preferred_element_type=jnp.float32) / math.sqrt(D)
    ).astype(jnp.bfloat16)
    up_delta = (
        lax.dot_general(up_grad, normed, TN, preferred_element_type=jnp.float32) / math.sqrt(D)
    ).astype(jnp.bfloat16)
    summed = jnp.stack(
        [
            module_sums(weighting, to_paths(delta.reshape(piece_shape)))
            for delta in (gate_delta, up_delta, down_delta)
        ],
        axis=1,
    )
    summed = summed.reshape(module_count, 3, block_rows, width)
    mean_delta = summed / counts[:, None, None, None]
    new_momentum = 0.9 * momentum + mean_delta
    new_params = (params.astype(jnp.float32) - 0.7 * (mean_delta + 0.9 * new_momentum)).astype(
        jnp.bfloat16
    )
    return (new_params, new_momentum)


def per_device(hidden_in, teacher, params, momentum, path_alive, path_module):
    token_rows = 3 * hidden_in.shape[0] * lax.axis_size("path") * lax.axis_size("tensor")
    weight_rows = 2 * params.shape[1] * params.shape[2] * lax.axis_size("path")
    body = tokens_move if token_rows <= weight_rows else weights_move
    return body(hidden_in, teacher, params, momentum, path_alive, path_module)


def solution(mesh):
    return jax.shard_map(
        per_device,
        mesh=mesh,
        in_specs=(
            P(BOTH, None),
            P("path", None),
            P(None, None, ("tensor", "path"), None),
            P(None, None, ("tensor", "path"), None),
            P(),
            P(),
        ),
        out_specs=(
            P(None, None, ("tensor", "path"), None),
            P(None, None, ("tensor", "path"), None),
        ),
        check_vma=False,
    )
```

```python
import functools
import math

import jax
import jax.numpy as jnp
from jax import lax
from jax.experimental import pallas as pl
from jax.experimental.pallas import tpu as pltpu
from jax.sharding import PartitionSpec as P

D = 2048
FW = 7168
NT = (((1,), (1,)), ((), ()))
TN = (((0,), (0,)), ((), ()))
BOTH = ("path", "tensor")
EACH_VMEM = 56 * 1024 * 1024


def rms(rows):
    wide = rows.astype(jnp.float32)
    mean_sq = jnp.mean(jnp.square(wide), axis=1, keepdims=True)
    return (wide * lax.rsqrt(mean_sq + 1e-05)).astype(jnp.bfloat16)


def forward_kernel(order, module, slot, z_ref, w_ref, part_ref, gate_ref, up_ref):
    z = z_ref[...]
    gate = lax.dot_general(w_ref[0, 0], z, NT, preferred_element_type=jnp.float32) / math.sqrt(D)
    up = lax.dot_general(w_ref[0, 1], z, NT, preferred_element_type=jnp.float32) / math.sqrt(D)
    gate_ref[0] = gate
    up_ref[0] = up
    hidden = (gate * jax.nn.sigmoid(gate) * up).astype(jnp.bfloat16)
    out = lax.dot_general(hidden, w_ref[0, 2], TN, preferred_element_type=jnp.float32)
    part_ref[...] = (out / math.sqrt(FW)).astype(part_ref.dtype)


def forward(order, module, slot, normed, params):
    paths = order.shape[0]
    tok = normed.shape[0] // paths
    _, kinds, rows, width = params.shape
    saved = jax.ShapeDtypeStruct((paths, rows, tok), jnp.float32)
    saved_spec = pl.BlockSpec((1, rows, tok), lambda j, o, m, s: (o[j], 0, 0))
    return pl.pallas_call(
        forward_kernel,
        grid_spec=pltpu.PrefetchScalarGridSpec(
            num_scalar_prefetch=3,
            grid=(paths,),
            in_specs=[
                pl.BlockSpec((tok, width), lambda j, o, m, s: (o[j], 0)),
                pl.BlockSpec((1, kinds, rows, width), lambda j, o, m, s: (m[j], 0, 0, 0)),
            ],
            out_specs=[
                pl.BlockSpec((tok, width), lambda j, o, m, s: (s[j], 0)),
                saved_spec,
                saved_spec,
            ],
        ),
        out_shape=[
            jax.ShapeDtypeStruct((paths * tok, width), PART),
            saved,
            saved,
        ],
        compiler_params=pltpu.CompilerParams(vmem_limit_bytes=EACH_VMEM),
    )(order, module, slot, normed, params)


def backward_kernel(
    order, module, alive, first, last, scale,
    z_ref, cot_ref, gate_ref, up_ref, w_ref, mom_ref, new_w_ref, new_mom_ref, total,
):
    j = pl.program_id(0)

    @pl.when(first[j] == 1)
    def _():
        total[...] = jnp.zeros_like(total)

    @pl.when(alive[j] == 1)
    def _():
        z = z_ref[...]
        cot = cot_ref[...]
        gate = gate_ref[0]
        up = up_ref[0]
        grad = lax.dot_general(w_ref[0, 2], cot, NT, preferred_element_type=jnp.float32)
        grad = grad / math.sqrt(FW)
        sig = jax.nn.sigmoid(gate)
        act = gate * sig
        gate_grad = (grad * up * sig * (1.0 + gate * (1.0 - sig))).astype(jnp.bfloat16)
        up_grad = (grad * act).astype(jnp.bfloat16)
        hidden = (act * up).astype(jnp.bfloat16)

        def add(kind, left, right, factor):
            delta = jnp.dot(left, right, preferred_element_type=jnp.float32) / factor
            total[kind] += delta.astype(jnp.bfloat16).astype(jnp.float32)

        add(0, gate_grad, z, math.sqrt(D))
        add(1, up_grad, z, math.sqrt(D))
        add(2, hidden, cot, math.sqrt(FW))

    @pl.when(last[j] == 1)
    def _():
        mean = total[...] / scale[module[j]]
        new_mom = 0.9 * mom_ref[0] + mean
        new_mom_ref[0] = new_mom
        new_w_ref[0] = (w_ref[0].astype(jnp.float32) - 0.7 * (mean + 0.9 * new_mom)).astype(
            jnp.bfloat16
        )


def backward(order, module, alive, first, last, counts, normed, cot, gate, up, params, momentum):
    paths = order.shape[0]
    tok = normed.shape[0] // paths
    _, kinds, rows, width = params.shape
    row_spec = pl.BlockSpec((tok, width), lambda j, o, m, *_: (o[j], 0))
    saved_spec = pl.BlockSpec((1, rows, tok), lambda j, o, m, *_: (o[j], 0, 0))
    own_spec = pl.BlockSpec((1, kinds, rows, width), lambda j, o, m, *_: (m[j], 0, 0, 0))
    return pl.pallas_call(
        backward_kernel,
        grid_spec=pltpu.PrefetchScalarGridSpec(
            num_scalar_prefetch=6,
            grid=(paths,),
            in_specs=[row_spec, row_spec, saved_spec, saved_spec, own_spec, own_spec],
            out_specs=[own_spec, own_spec],
            scratch_shapes=[pltpu.VMEM((kinds, rows, width), jnp.float32)],
        ),
        out_shape=[
            jax.ShapeDtypeStruct(params.shape, jnp.bfloat16),
            jax.ShapeDtypeStruct(momentum.shape, jnp.float32),
        ],
        compiler_params=pltpu.CompilerParams(vmem_limit_bytes=EACH_VMEM),
    )(order, module, alive, first, last, counts, normed, cot, gate, up, params, momentum)


PART = jnp.bfloat16


def plan_order(path_alive, path_module, module_count):
    paths = path_alive.shape[0]
    index = jnp.arange(paths, dtype=jnp.int32)
    key = path_module * paths + index
    rank = jnp.sum((key[None, :] < key[:, None]).astype(jnp.int32), axis=1)
    at = (rank[None, :] == index[:, None]).astype(jnp.int32)
    order = jnp.sum(at * index[None, :], axis=1)
    module = jnp.sum(at * path_module[None, :], axis=1)
    alive = jnp.sum(at * path_alive[None, :], axis=1)
    edge = jnp.ones((1,), jnp.int32)
    change = (module[1:] != module[:-1]).astype(jnp.int32)
    first = jnp.concatenate([edge, change])
    last = jnp.concatenate([change, edge])
    member = (path_module[:, None] == jnp.arange(module_count, dtype=jnp.int32)[None, :]).astype(
        jnp.int32
    ) * path_alive[:, None]
    counts = jnp.sum(member, axis=0).astype(jnp.float32)
    return order, module, alive, first, last, counts


MESH = pl.DeviceIdType.MESH
ROUTES = ("xyz", "zxy", "zyx")


def flip(path, unit):
    return path + unit - 2 * unit * lax.rem(path // unit, 2)


def both(left, right):
    if left is None or right is None:
        return right if left is None else left
    return jnp.logical_and(left, right)


def guarded(condition, action):
    if condition is None:
        action()
    else:
        pl.when(condition)(action)


def gather_kernel(depth, own_ref, all_ref, local_sem, send_sem, recv_sem):
    path = lax.axis_index("path")
    z = lax.axis_index("tensor")
    piece = own_ref.shape[0] // len(ROUTES)
    hop = {"x": (flip(path, 2), z), "y": (flip(path, 4), z)}
    sibling = (flip(path, 1), z)
    up, down = (path, z + 1), (path, z - 1)
    has_up, has_down = z < depth - 1, z > 0

    barrier = pltpu.get_barrier_semaphore()

    def greet(device):
        pl.semaphore_signal(barrier, inc=1, device_id=device, device_id_type=MESH)

    for device in (hop["x"], hop["y"], sibling):
        greet(device)
    pl.when(has_up)(lambda: greet(up))
    pl.when(has_down)(lambda: greet(down))
    ends = (2 * depth - 3 - z) // (depth - 1) + (z + depth - 2) // (depth - 1)
    pl.semaphore_wait(barrier, 3 + ends)

    def place(origin, level, k):
        return all_ref.at[origin, level, pl.ds(k * piece, piece)]

    def copy(origin, level, k, slot, device, own):
        source = own_ref.at[pl.ds(k * piece, piece)] if own else place(origin, level, k)
        return pltpu.make_async_remote_copy(
            src_ref=source,
            dst_ref=place(origin, level, k),
            send_sem=send_sem.at[slot],
            recv_sem=recv_sem.at[(origin * depth + level) * len(ROUTES) + k],
            device_id=device,
            device_id_type=MESH,
        )

    def origin_of(base, dx, dy):
        base = flip(base, 2) if dx else base
        return flip(base, 4) if dy else base

    def valid(s):
        if s == 0:
            return None
        return z >= -s if s < 0 else z < depth - s

    units = []
    for k, route in enumerate(ROUTES):
        for dx in range(2):
            for dy in range(2):
                for s in range(1 - depth, depth):
                    moved = {"x": dx, "y": dy, "z": abs(s)}
                    load = sum(moved.values()) + (1 if route[0] == "x" and s else 0)
                    units.append((load, k, dx, dy, s))
    units.sort()

    sent = []

    def send(condition, origin, level, k, device, own):
        slot = len(sent)
        sent.append((condition, origin, level, k, device, own))
        guarded(condition, lambda: copy(origin, level, k, slot, device, own).start())

    for _, k, dx, dy, s in units:
        route = ROUTES[k]
        moved = {"x": dx, "y": dy, "z": abs(s)}
        used = [i for i, axis in enumerate(route) if moved[axis]]
        own = not used
        here = valid(s)
        origin, level = origin_of(path, dx, dy), z + s
        if not own:
            guarded(here, lambda: copy(origin, level, k, 0, sibling, False).wait_recv())
        at = used[-1] if used else -1
        if at >= 0 and route[at] == "z":
            if s < 0 and -s < depth - 1:
                send(both(here, has_up), origin, level, k, up, own)
            if s > 0 and s < depth - 1:
                send(both(here, has_down), origin, level, k, down, own)
        for axis in route[at + 1:]:
            if axis == "z":
                send(both(here, has_up), origin, level, k, up, own)
                send(both(here, has_down), origin, level, k, down, own)
            else:
                send(here, origin, level, k, hop[axis], own)
        send(here, origin, level, k, sibling, own)

    keep = pltpu.make_async_copy(own_ref, all_ref.at[path, z], local_sem)
    keep.start()
    for _, k, dx, dy, s in units:
        origin, level = origin_of(sibling[0], dx, dy), z + s
        guarded(valid(s), lambda: copy(origin, level, k, 0, sibling, False).wait_recv())
    for slot, (condition, origin, level, k, device, own) in enumerate(sent):
        guarded(condition, lambda: copy(origin, level, k, slot, device, own).wait_send())
    keep.wait()


def gather_rows(own, collective_id):
    paths, depth = lax.axis_size("path"), lax.axis_size("tensor")
    rows, width = own.shape
    kinds = len(ROUTES)
    slots = kinds * 4 * (2 * depth - 1) * 3
    whole = pl.pallas_call(
        functools.partial(gather_kernel, depth),
        out_shape=jax.ShapeDtypeStruct((paths, depth, rows, width), own.dtype),
        in_specs=[pl.BlockSpec(memory_space=pl.ANY)],
        out_specs=pl.BlockSpec(memory_space=pl.ANY),
        scratch_shapes=[
            pltpu.SemaphoreType.DMA,
            pltpu.SemaphoreType.DMA((slots,)),
            pltpu.SemaphoreType.DMA((paths * depth * kinds,)),
        ],
        compiler_params=pltpu.CompilerParams(
            collective_id=collective_id, has_side_effects=True
        ),
    )(own)
    return whole.reshape(paths * depth * rows, width)


SPLIT = (("xylh", 5), ("yxlh", 5), ("lhxy", 2))
AXES = {"x": ("path", 2), "y": ("path", 4), "l": ("tensor", 1), "h": ("tensor", 2)}


def swap(away, axis, distance):
    size = lax.axis_size(axis)
    pairs = [(i, i + distance - 2 * distance * (i // distance % 2)) for i in range(size)]
    return lax.ppermute(away, axis, pairs)


def add(keep, came):
    return (keep.astype(jnp.float32) + came.astype(jnp.float32)).astype(keep.dtype)


def scatter_rows(part, share):
    width = part.shape[1]
    value = part.reshape(2, 2, 2, 2, 2, share, width)
    value = add(value[0], swap(value[1], "path", 1))
    step = share // sum(weight for _, weight in SPLIT)
    pieces, start = [], 0
    for _, weight in SPLIT:
        pieces.append(value[..., start:start + weight * step, :])
        start += weight * step
    names = [["y", "x", "h", "l"] for _ in SPLIT]
    for turn in range(4):
        keeps, aways = [], []
        for piece, left, (route, _) in zip(pieces, names, SPLIT):
            mesh_axis, distance = AXES[route[turn]]
            dim = left.index(route[turn])
            bit = lax.rem(lax.axis_index(mesh_axis) // distance, 2)
            keeps.append(lax.dynamic_index_in_dim(piece, bit, dim, keepdims=False))
            aways.append(lax.dynamic_index_in_dim(piece, 1 - bit, dim, keepdims=False))
            left.remove(route[turn])
        aways = lax.optimization_barrier(aways)
        came = [swap(a, *AXES[route[turn]]) for a, (route, _) in zip(aways, SPLIT)]
        came = lax.optimization_barrier(came)
        pieces = [add(k, c) for k, c in zip(keeps, came)]
    return jnp.concatenate(pieces, axis=0)


def tokens_move(hidden_in, teacher, params, momentum, path_alive, path_module):
    order, module, alive, first, last, counts = plan_order(
        path_alive, path_module, params.shape[0]
    )
    share = hidden_in.shape[0]
    normed = gather_rows(rms(hidden_in), 0)
    half = order.shape[0] // 2
    other = (order + lax.axis_index("path")) % 2
    part, gate, up = forward(order, module, other * half + order // 2, normed, params)
    output = scatter_rows(part, share)
    own = lax.dynamic_slice_in_dim(teacher, lax.axis_index("tensor") * share, share, 0)
    cot_share = (4.0 * (output.astype(jnp.float32) - own.astype(jnp.float32))).astype(jnp.bfloat16)
    cot = gather_rows(cot_share, 0)
    return tuple(
        backward(
            order, module, alive, first, last, counts, normed, cot, gate, up, params, momentum
        )
    )


def module_sums(weighting, received):
    flat = received.reshape(received.shape[0], -1)
    return lax.dot_general(weighting, flat, TN, preferred_element_type=jnp.float32)


def pick(stacked, path_module):
    index = path_module[:, None, None]
    chosen = jnp.broadcast_to(stacked[0][None], (path_module.shape[0],) + stacked.shape[1:])
    for m in range(1, stacked.shape[0]):
        chosen = jnp.where(index == m, stacked[m][None], chosen)
    return chosen


def weights_move(hidden_in, teacher, params, momentum, path_alive, path_module):
    module_count = params.shape[0]
    block_rows = params.shape[2]
    width = params.shape[3]
    path_count = path_alive.shape[0]
    n_tensor = lax.axis_size("tensor")

    def to_paths(x):
        return lax.all_to_all(x, "path", split_axis=0, concat_axis=0, tiled=True)

    local_rows = path_count * block_rows
    gate_rows, up_rows, down_rows = (
        to_paths(pick(params[:, k], path_module)).reshape(local_rows, width) for k in range(3)
    )
    normed = rms(lax.all_gather(hidden_in, "tensor", axis=0, tiled=True))
    gate_pre = lax.dot_general(
        normed, gate_rows, NT, preferred_element_type=jnp.float32
    ) / math.sqrt(D)
    up_proj = lax.dot_general(normed, up_rows, NT, preferred_element_type=jnp.float32) / math.sqrt(
        D
    )
    sigmoid_gate = jax.nn.sigmoid(gate_pre)
    activated = gate_pre * sigmoid_gate
    hidden = (activated * up_proj).astype(jnp.bfloat16)
    share_rows = teacher.shape[0] // n_tensor
    output_share = lax.psum_scatter(
        jnp.dot(hidden, down_rows, preferred_element_type=jnp.float32) / math.sqrt(FW),
        "tensor",
        scatter_dimension=0,
        tiled=True,
    )
    own_rows = lax.dynamic_slice_in_dim(
        teacher, lax.axis_index("tensor") * share_rows, share_rows, 0
    )
    cotangent_share = (4.0 * (output_share - own_rows.astype(jnp.float32))).astype(jnp.bfloat16)
    cotangent = lax.all_gather(cotangent_share, "tensor", axis=0, tiled=True)
    down_delta = (
        lax.dot_general(hidden, cotangent, TN, preferred_element_type=jnp.float32) / math.sqrt(FW)
    ).astype(jnp.bfloat16)
    hidden_grad = lax.dot_general(
        cotangent, down_rows, NT, preferred_element_type=jnp.float32
    ) / math.sqrt(FW)
    gate_grad = (
        hidden_grad * up_proj * sigmoid_gate * (1.0 + gate_pre * (1.0 - sigmoid_gate))
    ).astype(jnp.bfloat16)
    up_grad = (hidden_grad * activated).astype(jnp.bfloat16)
    member = (path_module[:, None] == jnp.arange(module_count, dtype=jnp.int32)[None, :]).astype(
        jnp.int32
    ) * path_alive[:, None]
    weighting = member.astype(jnp.bfloat16)
    counts = jnp.sum(member, axis=0).astype(jnp.float32)
    piece_shape = (path_count, block_rows, width)
    gate_delta = (
        lax.dot_general(gate_grad, normed, TN, preferred_element_type=jnp.float32) / math.sqrt(D)
    ).astype(jnp.bfloat16)
    up_delta = (
        lax.dot_general(up_grad, normed, TN, preferred_element_type=jnp.float32) / math.sqrt(D)
    ).astype(jnp.bfloat16)
    summed = jnp.stack(
        [
            module_sums(weighting, to_paths(delta.reshape(piece_shape)))
            for delta in (gate_delta, up_delta, down_delta)
        ],
        axis=1,
    )
    summed = summed.reshape(module_count, 3, block_rows, width)
    mean_delta = summed / counts[:, None, None, None]
    new_momentum = 0.9 * momentum + mean_delta
    new_params = (params.astype(jnp.float32) - 0.7 * (mean_delta + 0.9 * new_momentum)).astype(
        jnp.bfloat16
    )
    return (new_params, new_momentum)


def per_device(hidden_in, teacher, params, momentum, path_alive, path_module):
    token_rows = 3 * hidden_in.shape[0] * lax.axis_size("path") * lax.axis_size("tensor")
    weight_rows = 2 * params.shape[1] * params.shape[2] * lax.axis_size("path")
    small = lax.axis_size("path") == 8 and lax.axis_size("tensor") == 4 and token_rows <= weight_rows
    body = tokens_move if small else weights_move
    return body(hidden_in, teacher, params, momentum, path_alive, path_module)


def solution(mesh):
    return jax.shard_map(
        per_device,
        mesh=mesh,
        in_specs=(
            P(BOTH, None),
            P("path", None),
            P(None, None, ("tensor", "path"), None),
            P(None, None, ("tensor", "path"), None),
            P(),
            P(),
        ),
        out_specs=(
            P(None, None, ("tensor", "path"), None),
            P(None, None, ("tensor", "path"), None),
        ),
        check_vma=False,
    )
```

```python
import functools
import math

import jax
import jax.numpy as jnp
from jax import lax
from jax.experimental import pallas as pl
from jax.experimental.pallas import tpu as pltpu
from jax.sharding import PartitionSpec as P

D = 2048
FW = 7168
NT = (((1,), (1,)), ((), ()))
TN = (((0,), (0,)), ((), ()))
BOTH = ("path", "tensor")
EACH_VMEM = 56 * 1024 * 1024


def rms(rows):
    wide = rows.astype(jnp.float32)
    mean_sq = jnp.mean(jnp.square(wide), axis=1, keepdims=True)
    return (wide * lax.rsqrt(mean_sq + 1e-05)).astype(jnp.bfloat16)


def forward_kernel(order, module, z_ref, w_ref, part_ref, gate_ref, up_ref):
    z = z_ref[...]
    gate = lax.dot_general(w_ref[0, 0], z, NT, preferred_element_type=jnp.float32) / math.sqrt(D)
    up = lax.dot_general(w_ref[0, 1], z, NT, preferred_element_type=jnp.float32) / math.sqrt(D)
    gate_ref[0] = gate
    up_ref[0] = up
    hidden = (gate * jax.nn.sigmoid(gate) * up).astype(jnp.bfloat16)
    out = lax.dot_general(hidden, w_ref[0, 2], TN, preferred_element_type=jnp.float32)
    part_ref[...] = (out / math.sqrt(FW)).astype(part_ref.dtype)


def forward(order, module, tok, normed, params):
    paths = order.shape[0]
    _, kinds, rows, width = params.shape
    saved = jax.ShapeDtypeStruct((paths, rows, tok), jnp.float32)
    saved_spec = pl.BlockSpec((1, rows, tok), lambda j, o, m: (j, 0, 0))
    return pl.pallas_call(
        forward_kernel,
        grid_spec=pltpu.PrefetchScalarGridSpec(
            num_scalar_prefetch=2,
            grid=(paths,),
            in_specs=[
                pl.BlockSpec((tok, width), lambda j, o, m: (o[j], 0)),
                pl.BlockSpec((1, kinds, rows, width), lambda j, o, m: (m[j], 0, 0, 0)),
            ],
            out_specs=[
                pl.BlockSpec((tok, width), lambda j, o, m: (j, 0)),
                saved_spec,
                saved_spec,
            ],
        ),
        out_shape=[
            jax.ShapeDtypeStruct((paths * tok, width), PART),
            saved,
            saved,
        ],
        cost_estimate=pl.CostEstimate(
            flops=2 * kinds * paths * tok * rows * width,
            bytes_accessed=paths * (4 * tok * width + 8 * rows * tok + 2 * kinds * rows * width),
            transcendentals=paths * rows * tok,
        ),
        compiler_params=pltpu.CompilerParams(vmem_limit_bytes=EACH_VMEM),
    )(order, module, normed, params)


def backward_kernel(
    order, module, alive, first, last, scale, slot,
    z_ref, cot_ref, gate_ref, up_ref, w_ref, mom_ref, new_w_ref, new_mom_ref, total,
):
    j = pl.program_id(0)

    @pl.when(first[j] == 1)
    def _():
        total[...] = jnp.zeros_like(total)

    @pl.when(alive[j] == 1)
    def _():
        z = z_ref[...]
        cot = cot_ref[...]
        gate = gate_ref[0]
        up = up_ref[0]
        grad = lax.dot_general(w_ref[0, 2], cot, NT, preferred_element_type=jnp.float32)
        grad = grad / math.sqrt(FW)
        sig = jax.nn.sigmoid(gate)
        act = gate * sig
        gate_grad = (grad * up * sig * (1.0 + gate * (1.0 - sig))).astype(jnp.bfloat16)
        up_grad = (grad * act).astype(jnp.bfloat16)
        hidden = (act * up).astype(jnp.bfloat16)

        def add(kind, left, right, factor):
            delta = jnp.dot(left, right, preferred_element_type=jnp.float32) / factor
            total[kind] += delta.astype(jnp.bfloat16).astype(jnp.float32)

        add(0, gate_grad, z, math.sqrt(D))
        add(1, up_grad, z, math.sqrt(D))
        add(2, hidden, cot, math.sqrt(FW))

    @pl.when(last[j] == 1)
    def _():
        mean = total[...] / scale[module[j]]
        new_mom = 0.9 * mom_ref[0] + mean
        new_mom_ref[0] = new_mom
        new_w_ref[0] = (w_ref[0].astype(jnp.float32) - 0.7 * (mean + 0.9 * new_mom)).astype(
            jnp.bfloat16
        )


def backward(order, module, alive, first, last, counts, slot, normed, cot, gate, up, params, momentum):
    paths = order.shape[0]
    tok = normed.shape[0] // paths
    _, kinds, rows, width = params.shape
    row_spec = pl.BlockSpec((tok, width), lambda j, o, m, *_: (o[j], 0))
    saved_spec = pl.BlockSpec((1, rows, tok), lambda j, o, m, a, f, l, c, s: (s[j], 0, 0))
    own_spec = pl.BlockSpec((1, kinds, rows, width), lambda j, o, m, *_: (m[j], 0, 0, 0))
    return pl.pallas_call(
        backward_kernel,
        grid_spec=pltpu.PrefetchScalarGridSpec(
            num_scalar_prefetch=7,
            grid=(paths,),
            in_specs=[row_spec, row_spec, saved_spec, saved_spec, own_spec, own_spec],
            out_specs=[own_spec, own_spec],
            scratch_shapes=[pltpu.VMEM((kinds, rows, width), jnp.float32)],
        ),
        out_shape=[
            jax.ShapeDtypeStruct(params.shape, jnp.bfloat16),
            jax.ShapeDtypeStruct(momentum.shape, jnp.float32),
        ],
        compiler_params=pltpu.CompilerParams(vmem_limit_bytes=EACH_VMEM),
    )(order, module, alive, first, last, counts, slot, normed, cot, gate, up, params, momentum)


PART = jnp.bfloat16


def plan_order(path_alive, path_module, module_count):
    paths = path_alive.shape[0]
    index = jnp.arange(paths, dtype=jnp.int32)
    key = path_module * paths + index
    rank = jnp.sum((key[None, :] < key[:, None]).astype(jnp.int32), axis=1)
    at = (rank[None, :] == index[:, None]).astype(jnp.int32)
    order = jnp.sum(at * index[None, :], axis=1)
    module = jnp.sum(at * path_module[None, :], axis=1)
    alive = jnp.sum(at * path_alive[None, :], axis=1)
    edge = jnp.ones((1,), jnp.int32)
    change = (module[1:] != module[:-1]).astype(jnp.int32)
    first = jnp.concatenate([edge, change])
    last = jnp.concatenate([change, edge])
    member = (path_module[:, None] == jnp.arange(module_count, dtype=jnp.int32)[None, :]).astype(
        jnp.int32
    ) * path_alive[:, None]
    counts = jnp.sum(member, axis=0).astype(jnp.float32)
    return order, module, alive, first, last, counts


MESH = pl.DeviceIdType.MESH
ROUTES = ("xyz", "zxy", "zyx")


def flip(path, unit):
    return path + unit - 2 * unit * lax.rem(path // unit, 2)


def both(left, right):
    if left is None or right is None:
        return right if left is None else left
    return jnp.logical_and(left, right)


def guarded(condition, action):
    if condition is None:
        action()
    else:
        pl.when(condition)(action)


def gather_kernel(depth, own_ref, all_ref, local_sem, send_sem, recv_sem):
    path = lax.axis_index("path")
    z = lax.axis_index("tensor")
    piece = own_ref.shape[0] // len(ROUTES)
    hop = {"x": (flip(path, 2), z), "y": (flip(path, 4), z)}
    sibling = (flip(path, 1), z)
    up, down = (path, z + 1), (path, z - 1)
    has_up, has_down = z < depth - 1, z > 0

    barrier = pltpu.get_barrier_semaphore()

    def greet(device):
        pl.semaphore_signal(barrier, inc=1, device_id=device, device_id_type=MESH)

    for device in (hop["x"], hop["y"], sibling):
        greet(device)
    pl.when(has_up)(lambda: greet(up))
    pl.when(has_down)(lambda: greet(down))
    ends = (2 * depth - 3 - z) // (depth - 1) + (z + depth - 2) // (depth - 1)
    pl.semaphore_wait(barrier, 3 + ends)

    def place(origin, level, k):
        return all_ref.at[origin, level, pl.ds(k * piece, piece)]

    def copy(origin, level, k, slot, device, own):
        source = own_ref.at[pl.ds(k * piece, piece)] if own else place(origin, level, k)
        return pltpu.make_async_remote_copy(
            src_ref=source,
            dst_ref=place(origin, level, k),
            send_sem=send_sem.at[slot],
            recv_sem=recv_sem.at[(origin * depth + level) * len(ROUTES) + k],
            device_id=device,
            device_id_type=MESH,
        )

    def origin_of(base, dx, dy):
        base = flip(base, 2) if dx else base
        return flip(base, 4) if dy else base

    def valid(s):
        if s == 0:
            return None
        return z >= -s if s < 0 else z < depth - s

    units = []
    for k, route in enumerate(ROUTES):
        for dx in range(2):
            for dy in range(2):
                for s in range(1 - depth, depth):
                    moved = {"x": dx, "y": dy, "z": abs(s)}
                    load = sum(moved.values()) + (1 if route[0] == "x" and s else 0)
                    units.append((load, k, dx, dy, s))
    units.sort()

    sent = []

    def send(condition, origin, level, k, device, own):
        slot = len(sent)
        sent.append((condition, origin, level, k, device, own))
        guarded(condition, lambda: copy(origin, level, k, slot, device, own).start())

    for _, k, dx, dy, s in units:
        route = ROUTES[k]
        moved = {"x": dx, "y": dy, "z": abs(s)}
        used = [i for i, axis in enumerate(route) if moved[axis]]
        own = not used
        here = valid(s)
        origin, level = origin_of(path, dx, dy), z + s
        if not own:
            guarded(here, lambda: copy(origin, level, k, 0, sibling, False).wait_recv())
        at = used[-1] if used else -1
        if at >= 0 and route[at] == "z":
            if s < 0 and -s < depth - 1:
                send(both(here, has_up), origin, level, k, up, own)
            if s > 0 and s < depth - 1:
                send(both(here, has_down), origin, level, k, down, own)
        for axis in route[at + 1:]:
            if axis == "z":
                send(both(here, has_up), origin, level, k, up, own)
                send(both(here, has_down), origin, level, k, down, own)
            else:
                send(here, origin, level, k, hop[axis], own)
        send(here, origin, level, k, sibling, own)

    keep = pltpu.make_async_copy(own_ref, all_ref.at[path, z], local_sem)
    keep.start()
    for _, k, dx, dy, s in units:
        origin, level = origin_of(sibling[0], dx, dy), z + s
        guarded(valid(s), lambda: copy(origin, level, k, 0, sibling, False).wait_recv())
    for slot, (condition, origin, level, k, device, own) in enumerate(sent):
        guarded(condition, lambda: copy(origin, level, k, slot, device, own).wait_send())
    keep.wait()


def gather_rows(own, collective_id):
    paths, depth = lax.axis_size("path"), lax.axis_size("tensor")
    rows, width = own.shape
    kinds = len(ROUTES)
    slots = kinds * 4 * (2 * depth - 1) * 3
    whole = pl.pallas_call(
        functools.partial(gather_kernel, depth),
        out_shape=jax.ShapeDtypeStruct((paths, depth, rows, width), own.dtype),
        in_specs=[pl.BlockSpec(memory_space=pl.ANY)],
        out_specs=pl.BlockSpec(memory_space=pl.ANY),
        scratch_shapes=[
            pltpu.SemaphoreType.DMA,
            pltpu.SemaphoreType.DMA((slots,)),
            pltpu.SemaphoreType.DMA((paths * depth * kinds,)),
        ],
        compiler_params=pltpu.CompilerParams(
            collective_id=collective_id, has_side_effects=True
        ),
    )(own)
    return whole.reshape(paths * depth * rows, width)


SPLIT = (("xylh", 5), ("yxlh", 5), ("lhxy", 2))
AXES = {"x": ("path", 2), "y": ("path", 4), "l": ("tensor", 1), "h": ("tensor", 2)}


def swap(away, axis, distance):
    size = lax.axis_size(axis)
    pairs = [(i, i + distance - 2 * distance * (i // distance % 2)) for i in range(size)]
    return lax.ppermute(away, axis, pairs)


def add(keep, came):
    return (keep.astype(jnp.float32) + came.astype(jnp.float32)).astype(keep.dtype)


def scatter_rows(keep, came, share):
    width = keep.shape[1]
    value = add(keep, came).reshape(2, 2, 2, 2, share, width)
    step = share // sum(weight for _, weight in SPLIT)
    pieces, start = [], 0
    for _, weight in SPLIT:
        pieces.append(value[..., start:start + weight * step, :])
        start += weight * step
    names = [["y", "x", "h", "l"] for _ in SPLIT]
    for turn in range(4):
        keeps, aways = [], []
        for piece, left, (route, _) in zip(pieces, names, SPLIT):
            mesh_axis, distance = AXES[route[turn]]
            dim = left.index(route[turn])
            bit = lax.rem(lax.axis_index(mesh_axis) // distance, 2)
            keeps.append(lax.dynamic_index_in_dim(piece, bit, dim, keepdims=False))
            aways.append(lax.dynamic_index_in_dim(piece, 1 - bit, dim, keepdims=False))
            left.remove(route[turn])
        aways = lax.optimization_barrier(aways)
        came = [swap(a, *AXES[route[turn]]) for a, (route, _) in zip(aways, SPLIT)]
        came = lax.optimization_barrier(came)
        pieces = [add(k, c) for k, c in zip(keeps, came)]
    return jnp.concatenate(pieces, axis=0)


def tokens_move(hidden_in, teacher, params, momentum, path_alive, path_module):
    order, module, alive, first, last, counts = plan_order(
        path_alive, path_module, params.shape[0]
    )
    share = hidden_in.shape[0]
    normed = gather_rows(rms(hidden_in), 0)
    half = order.shape[0] // 2
    core = lax.axis_index("path") % 2
    slot = ((order + core) % 2) * half + order // 2
    index = jnp.arange(2 * half, dtype=jnp.int32)

    def run(side):
        chosen = 2 * jnp.arange(half, dtype=jnp.int32) + side
        at = (chosen[:, None] == index[None, :]).astype(jnp.int32)
        which = jnp.sum(at * path_module[None, :], axis=1)
        return forward(chosen, which, teacher.shape[0], normed, params)

    away, away_gate, away_up = run(1 - core)
    came = swap(away, "path", 1)
    keep, keep_gate, keep_up = run(core)
    gate = jnp.concatenate([keep_gate, away_gate])
    up = jnp.concatenate([keep_up, away_up])
    output = scatter_rows(keep, came, share)
    own = lax.dynamic_slice_in_dim(teacher, lax.axis_index("tensor") * share, share, 0)
    cot_share = (4.0 * (output.astype(jnp.float32) - own.astype(jnp.float32))).astype(jnp.bfloat16)
    cot = gather_rows(cot_share, 0)
    return tuple(
        backward(
            order, module, alive, first, last, counts, slot, normed, cot, gate, up, params, momentum
        )
    )


def module_sums(weighting, received):
    flat = received.reshape(received.shape[0], -1)
    return lax.dot_general(weighting, flat, TN, preferred_element_type=jnp.float32)


def pick(stacked, path_module):
    index = path_module[:, None, None]
    chosen = jnp.broadcast_to(stacked[0][None], (path_module.shape[0],) + stacked.shape[1:])
    for m in range(1, stacked.shape[0]):
        chosen = jnp.where(index == m, stacked[m][None], chosen)
    return chosen


def weights_move(hidden_in, teacher, params, momentum, path_alive, path_module):
    module_count = params.shape[0]
    block_rows = params.shape[2]
    width = params.shape[3]
    path_count = path_alive.shape[0]
    n_tensor = lax.axis_size("tensor")

    def to_paths(x):
        return lax.all_to_all(x, "path", split_axis=0, concat_axis=0, tiled=True)

    local_rows = path_count * block_rows
    gate_rows, up_rows, down_rows = (
        to_paths(pick(params[:, k], path_module)).reshape(local_rows, width) for k in range(3)
    )
    normed = rms(lax.all_gather(hidden_in, "tensor", axis=0, tiled=True))
    gate_pre = lax.dot_general(
        normed, gate_rows, NT, preferred_element_type=jnp.float32
    ) / math.sqrt(D)
    up_proj = lax.dot_general(normed, up_rows, NT, preferred_element_type=jnp.float32) / math.sqrt(
        D
    )
    sigmoid_gate = jax.nn.sigmoid(gate_pre)
    activated = gate_pre * sigmoid_gate
    hidden = (activated * up_proj).astype(jnp.bfloat16)
    share_rows = teacher.shape[0] // n_tensor
    output_share = lax.psum_scatter(
        jnp.dot(hidden, down_rows, preferred_element_type=jnp.float32) / math.sqrt(FW),
        "tensor",
        scatter_dimension=0,
        tiled=True,
    )
    own_rows = lax.dynamic_slice_in_dim(
        teacher, lax.axis_index("tensor") * share_rows, share_rows, 0
    )
    cotangent_share = (4.0 * (output_share - own_rows.astype(jnp.float32))).astype(jnp.bfloat16)
    cotangent = lax.all_gather(cotangent_share, "tensor", axis=0, tiled=True)
    down_delta = (
        lax.dot_general(hidden, cotangent, TN, preferred_element_type=jnp.float32) / math.sqrt(FW)
    ).astype(jnp.bfloat16)
    hidden_grad = lax.dot_general(
        cotangent, down_rows, NT, preferred_element_type=jnp.float32
    ) / math.sqrt(FW)
    gate_grad = (
        hidden_grad * up_proj * sigmoid_gate * (1.0 + gate_pre * (1.0 - sigmoid_gate))
    ).astype(jnp.bfloat16)
    up_grad = (hidden_grad * activated).astype(jnp.bfloat16)
    member = (path_module[:, None] == jnp.arange(module_count, dtype=jnp.int32)[None, :]).astype(
        jnp.int32
    ) * path_alive[:, None]
    weighting = member.astype(jnp.bfloat16)
    counts = jnp.sum(member, axis=0).astype(jnp.float32)
    piece_shape = (path_count, block_rows, width)
    gate_delta = (
        lax.dot_general(gate_grad, normed, TN, preferred_element_type=jnp.float32) / math.sqrt(D)
    ).astype(jnp.bfloat16)
    up_delta = (
        lax.dot_general(up_grad, normed, TN, preferred_element_type=jnp.float32) / math.sqrt(D)
    ).astype(jnp.bfloat16)
    summed = jnp.stack(
        [
            module_sums(weighting, to_paths(delta.reshape(piece_shape)))
            for delta in (gate_delta, up_delta, down_delta)
        ],
        axis=1,
    )
    summed = summed.reshape(module_count, 3, block_rows, width)
    mean_delta = summed / counts[:, None, None, None]
    new_momentum = 0.9 * momentum + mean_delta
    new_params = (params.astype(jnp.float32) - 0.7 * (mean_delta + 0.9 * new_momentum)).astype(
        jnp.bfloat16
    )
    return (new_params, new_momentum)


def per_device(hidden_in, teacher, params, momentum, path_alive, path_module):
    token_rows = 3 * hidden_in.shape[0] * lax.axis_size("path") * lax.axis_size("tensor")
    weight_rows = 2 * params.shape[1] * params.shape[2] * lax.axis_size("path")
    small = lax.axis_size("path") == 8 and lax.axis_size("tensor") == 4 and token_rows <= weight_rows
    body = tokens_move if small else weights_move
    return body(hidden_in, teacher, params, momentum, path_alive, path_module)


def solution(mesh):
    return jax.shard_map(
        per_device,
        mesh=mesh,
        in_specs=(
            P(BOTH, None),
            P("path", None),
            P(None, None, ("tensor", "path"), None),
            P(None, None, ("tensor", "path"), None),
            P(),
            P(),
        ),
        out_specs=(
            P(None, None, ("tensor", "path"), None),
            P(None, None, ("tensor", "path"), None),
        ),
        check_vma=False,
    )
```
